32 devices in a mesh: blocks: 2 (over y), tile: 16 (over z, x, core).
Axes of the slice: x: 2, y: 2, z: 4, core: 2. Of those that a mesh axis runs over, the one named last changes fastest.
Arguments:
- raw_views: bfloat16 [8, 1024, 32, 128], P(None, ('blocks', 'tile')), parts along dimension 1, as said below
- spread_taps: float32 [8, 2, 3, 31], replicated, may hold values from 0.0001 to 1, as said below
Outputs:
- estimate: float32 [1024, 32, 128], P(('blocks', 'tile')), parts along dimension 0
The draws below stay inside these ranges and needn't reach their ends.
There are 2 independent parts, one for each index of `blocks`. The reference program is written for one: setup_inputs(seed, part) draws one part's arguments, and reference() takes and returns one part's arrays. A program takes and returns all parts, laid end to end along the dimension named above; an argument that names none is the same for every part. Nothing has to cross between parts.
Inputs may be any that keep to these rules, and one draw needn't show every extreme that they name: `raw_views`: every entry is positive. `spread_taps`: every tap is positive.
All inputs are finite; a program needn't handle non-finite values.
Results may differ from the reference program's by a relative error of at most 0.0031.
Values may be sent and summed in bfloat16 or wider, within the bound.
A program may use at most 64 MiB of HBM per device.

```python
import math
import jax
import jax.numpy as jnp
from jax import lax

VIEWS = 8
TAPS = 31
TERMS = 2
ITERS = 2
PLANES = 32
HEIGHT = 32
WIDTH = 128
RADIUS = 15
DEPTH = 512
N_TILE = 16


def draw_spread_taps(key, part):
    keys_all = jax.random.split(key, 2)
    offsets = jnp.arange(TAPS, dtype=jnp.float32) - RADIUS
    axis_widths = jnp.array([0.7, 0.35, 0.35], jnp.float32) * RADIUS
    broaden = 1.0 + 0.6 * jnp.arange(TERMS, dtype=jnp.float32)
    view_spread = jax.random.uniform(keys_all[0], (VIEWS, 1, 1), jnp.float32, 0.8, 1.25)
    spread_width = view_spread * axis_widths[None, None, :] * broaden[None, :, None]
    envelope = jnp.exp(-0.5 * (offsets / spread_width[..., None]) ** 2) / (spread_width[..., None] * 2.5066283)
    roughness = jax.random.uniform(keys_all[1], (VIEWS, TERMS, 3, TAPS), jnp.float32, 0.6, 1.4)
    term_weight = 0.35 ** jnp.arange(TERMS, dtype=jnp.float32)
    axis_first = (jnp.arange(3) == 0).astype(jnp.float32)
    weighting = axis_first[None, :] * term_weight[:, None] + (1.0 - axis_first[None, :])
    return jnp.clip(envelope * roughness * weighting[None, :, :, None], 0.0001, 1.0)


def draw_raw_views(key, part):
    keys_all = jax.random.split(key, 4)
    depth_pos = (jnp.arange(DEPTH, dtype=jnp.float32) + 0.5) / DEPTH
    alternate = jnp.arange(VIEWS, dtype=jnp.int32) % 2 * 2 - 1
    tilt_sign = jax.random.permutation(keys_all[0], alternate).astype(jnp.float32)
    gradient = math.log(3.0) + 0.5
    common_ramp = jnp.exp(gradient * depth_pos)
    tilt = jnp.exp(0.5 * tilt_sign[:, None] * (depth_pos[None, :] - 0.5) + 0.25)
    ramp = common_ramp[None, :] * tilt
    row_scale = jnp.exp(jax.random.uniform(keys_all[1], (DEPTH, HEIGHT), jnp.float32, math.log(0.3), math.log(3.0)))
    shared = jnp.exp(jax.random.uniform(keys_all[2], (DEPTH, HEIGHT, WIDTH), jnp.float32, -0.8, 0.8))
    own_part = jnp.exp(jax.random.uniform(keys_all[3], (VIEWS, DEPTH, HEIGHT, WIDTH), jnp.float32, -0.8, 0.8))
    mixture = 0.6 * shared[None] + 0.4 * own_part
    return (ramp[:, :, None, None] * row_scale[None, :, :, None] * mixture).astype(jnp.bfloat16)


def setup_inputs(seed: int = 0, part: int = 0) -> dict:
    seeds = jax.random.split(jax.random.key(seed), 3)
    part_keys = jax.random.split(jax.random.fold_in(seeds[2], part), 3)
    raw_views = draw_raw_views(jax.random.fold_in(jax.random.fold_in(seeds[2], part), 71), part)
    spread_taps = draw_spread_taps(jax.random.fold_in(seeds[2], 71), part)
    return {"raw_views": raw_views, "spread_taps": spread_taps}


def band_table(kernel_taps, length_in, length_out, tap_shift):
    tap_count = kernel_taps.shape[0]
    row_index = lax.broadcasted_iota(jnp.int32, (tap_count, length_in, length_out), 1)
    col_index = lax.broadcasted_iota(jnp.int32, (tap_count, length_in, length_out), 2)
    tap_index = lax.broadcasted_iota(jnp.int32, (tap_count, length_in, length_out), 0)
    selector = (row_index - col_index + tap_shift == tap_index).astype(jnp.float32)
    return jnp.einsum("k,kji->ji", kernel_taps.astype(jnp.float32), selector, precision=lax.Precision.HIGHEST)


def axis_depth(volume, kernel_taps):
    padded = jnp.pad(volume, ((RADIUS, RADIUS), (0, 0), (0, 0)))
    band_matrix = band_table(kernel_taps, PLANES + 2 * RADIUS, PLANES, 0)

    def one_block(start_plane):
        window_block = lax.dynamic_slice_in_dim(padded, start_plane, PLANES + 2 * RADIUS, 0)
        return jnp.einsum("jyx,ji->iyx", window_block.astype(jnp.float32), band_matrix)

    starts = jnp.arange(N_TILE, dtype=jnp.int32) * PLANES
    return lax.map(one_block, starts).reshape(DEPTH, HEIGHT, WIDTH)


def axis_height(volume, kernel_taps):
    band_matrix = band_table(kernel_taps, HEIGHT, HEIGHT, RADIUS)
    return jnp.einsum("zjx,ji->zix", volume.astype(jnp.float32), band_matrix)


def axis_width(volume, kernel_taps):
    band_matrix = band_table(kernel_taps, WIDTH, WIDTH, RADIUS)
    return jnp.einsum("zyj,ji->zyi", volume.astype(jnp.float32), band_matrix)


def blur(volume, kernel):
    summed = jnp.zeros(volume.shape, jnp.float32)
    for term_index in range(TERMS):
        first_pass = axis_depth(volume, kernel[term_index, 0]).astype(jnp.bfloat16)
        second = axis_height(first_pass, kernel[term_index, 1]).astype(jnp.bfloat16)
        summed = summed + axis_width(second, kernel[term_index, 2])
    return summed


def reference(raw_views, spread_taps):
    rounded_taps = spread_taps.astype(jnp.bfloat16)
    kernel = lax.optimization_barrier(rounded_taps).astype(jnp.float32)
    adjoint = kernel[:, :, :, ::-1]
    recorded = raw_views.astype(jnp.float32)
    totals = jnp.sum(recorded, axis=(1, 2, 3))
    scales = jnp.mean(totals) / totals
    scaled = recorded * scales[:, None, None, None]
    estimate = jnp.mean(scaled, axis=0)
    for iteration in range(ITERS):
        rounded = estimate.astype(jnp.bfloat16)
        factor = jnp.ones(estimate.shape, jnp.float32)
        for which_view in range(VIEWS):
            blurred = blur(rounded, kernel[which_view])
            quotient = (scaled[which_view] / blurred).astype(jnp.bfloat16)
            factor = factor * blur(quotient, adjoint[which_view])
        estimate = estimate * factor
    return estimate
```

```python
import functools

import jax
import jax.numpy as jnp
from jax import lax
from jax.experimental import pallas as pl
from jax.experimental.pallas import tpu as pltpu
from jax.sharding import PartitionSpec as P

ITERS = 2
SUB = 8
HALO = 16
F32 = jnp.float32
BF16 = jnp.bfloat16
MESH = pl.DeviceIdType.MESH


def dot(a, b):
    return jnp.dot(a, b, preferred_element_type=F32)


def kernel_body(
    n, radius, raw_in, taps, out, relay, raw, esto, estp, estn, est, fac, zin, qx,
    wxf, wxb, ykf, ykb, zf, zb, brow, tot, scl,
    tot_ss, tot_rs, raw_ss, raw_rs, est_ss, est_rs,
):
    views, planes, height, width = raw_in.shape
    terms = zb.shape[1] // planes
    me = lax.axis_index("tile")
    prev, nxt = lax.rem(me + n - 1, n), lax.rem(me + 1, n)
    has_prev, has_next = me > 0, me < n - 1
    groups = planes // SUB
    own = planes // HALO
    wide = own + 2

    barrier = pltpu.get_barrier_semaphore()

    def greet(i, c):
        pl.semaphore_signal(
            barrier, inc=1, device_id={"tile": lax.rem(me + i, n)}, device_id_type=MESH
        )
        return c

    lax.fori_loop(1, n, greet, 0)

    def relayout(v, c):
        for z in range(planes):
            relay[pl.ds(z, height, stride=planes), :] = raw_in[v, z].astype(F32)
        block = relay[...].reshape(height, planes, width)
        for k in range(own):
            raw[v, 1 + k] = block[:, k * HALO:(k + 1) * HALO, :].astype(BF16)
        tot[0, pl.ds(v, 1), :] = jnp.sum(relay[...], axis=0, keepdims=True)
        return c

    lax.fori_loop(0, views, relayout, 0)
    pl.semaphore_wait(barrier, n - 1)

    def tot_copy(i):
        return pltpu.make_async_remote_copy(
            src_ref=tot.at[0], dst_ref=tot.at[i], send_sem=tot_ss.at[i], recv_sem=tot_rs.at[i],
            device_id={"tile": lax.rem(me + i, n)}, device_id_type=MESH,
        )

    def tot_start(i, c):
        tot_copy(i).start()
        return c

    def tot_wait(i, c):
        tot_copy(i).wait()
        return c

    lax.fori_loop(1, n, tot_start, 0)

    def exchange(src_lo, dst_lo, src_hi, dst_hi, ss, rs):
        down = pltpu.make_async_remote_copy(
            src_ref=src_lo, dst_ref=dst_hi, send_sem=ss.at[0], recv_sem=rs.at[0],
            device_id={"tile": prev}, device_id_type=MESH,
        )
        up = pltpu.make_async_remote_copy(
            src_ref=src_hi, dst_ref=dst_lo, send_sem=ss.at[1], recv_sem=rs.at[1],
            device_id={"tile": nxt}, device_id_type=MESH,
        )

        def start():
            @pl.when(has_prev)
            def _():
                down.start()

            @pl.when(has_next)
            def _():
                up.start()

        def wait_recv():
            @pl.when(has_prev)
            def _():
                up.wait_recv()

            @pl.when(has_next)
            def _():
                down.wait_recv()

        def wait_send():
            @pl.when(has_prev)
            def _():
                down.wait_send()

            @pl.when(has_next)
            def _():
                up.wait_send()

        return start, wait_recv, wait_send

    raw_x = exchange(
        raw.at[:, 1], raw.at[:, 0], raw.at[:, own], raw.at[:, own + 1], raw_ss, raw_rs
    )
    est_x = [
        exchange(
            esto.at[i], estp.at[i], esto.at[i], estn.at[i], est_ss.at[i], est_rs.at[i]
        )
        for i in range(ITERS)
    ]
    raw_x[0]()

    @pl.when(me == 0)
    def _():
        estp[...] = jnp.zeros_like(estp)
        raw[:, 0] = jnp.zeros_like(raw[:, 0])

    @pl.when(me == n - 1)
    def _():
        estn[...] = jnp.zeros_like(estn)
        raw[:, own + 1] = jnp.zeros_like(raw[:, own + 1])

    lanes = taps.shape[1]
    tap = lax.broadcasted_iota(jnp.int32, (lanes, lanes), 0)
    lane = lax.broadcasted_iota(jnp.int32, (lanes, lanes), 1)
    signed = jnp.where(lane < lanes // 2, lane, lane - lanes)
    far = lane - lanes
    vt = views * terms

    def place(k, dim, wanted, keep=None):
        hit = tap == wanted
        if keep is not None:
            hit = jnp.logical_and(hit, keep)
        brow[k] = dot(taps[dim * vt:(dim + 1) * vt, :], hit.astype(F32).astype(BF16))

    step = lane % SUB == 0
    place(0, 2, radius - signed)
    place(1, 2, radius + signed)
    place(2, 1, lane // SUB + radius, step)
    place(3, 1, lane // SUB + radius - lanes // SUB, step)
    place(4, 1, radius - lane // SUB, step)
    place(5, 1, radius - lane // SUB + lanes // SUB, step)
    place(6, 0, lane - (HALO - radius))
    place(7, 0, 2 * radius + HALO - radius - lane)

    row = tap
    near = jnp.abs(row - lane) <= radius
    after = lane >= row

    def rolled(k, i, rows):
        line = jnp.broadcast_to(brow[k, pl.ds(i, 1), :], (rows, lanes))
        return pltpu.roll(line, 0, 1, stride=1, stride_axis=0)

    def tables(wx, yk, z, kx, ky, kz, zrows, zcols):
        def one(v, c):
            for t in range(terms):
                i = v * terms + t
                wx[v, t * width:(t + 1) * width, :] = jnp.where(
                    near, rolled(kx, i, width), 0.0
                ).astype(BF16)
                r0 = rolled(ky, i, lanes)
                r1 = rolled(ky + 1, i, lanes)
                t0 = jnp.where(after, r0, r1).astype(BF16)
                yk[i, 0:lanes, 0:lanes] = t0
                yk[i, lanes:2 * lanes, lanes:2 * lanes] = t0
                yk[i, 0:lanes, lanes:2 * lanes] = jnp.where(after, 0.0, r0).astype(BF16)
                yk[i, lanes:2 * lanes, 0:lanes] = jnp.where(after, r1, 0.0).astype(BF16)
                z[v, t * zrows:(t + 1) * zrows, :] = rolled(kz, i, zrows)[:, :zcols].astype(BF16)
            return c

        lax.fori_loop(0, views, one, 0)

    tables(wxf, ykf, zf, 0, 2, 6, wide * HALO, zf.shape[2])

    lax.fori_loop(1, n, tot_wait, 0)
    summed = lax.fori_loop(0, n, lambda i, a: a + tot[i], jnp.zeros(tot.shape[1:], F32))
    totals = jnp.sum(summed, axis=1, keepdims=True)
    mean = jnp.sum(totals, axis=0, keepdims=True) / views
    scl[...] = jnp.broadcast_to(mean / totals, scl.shape)

    chunk = SUB
    for k in range(own):
        def first(j, c):
            acc = jnp.zeros((chunk, HALO, width), F32)
            for v in range(views):
                s = scl[v:v + 1, :].reshape(1, 1, width)
                acc = acc + s * raw[v, 1 + k, pl.ds(j * chunk, chunk)].astype(F32)
            acc = acc / views
            for h in range(HALO // SUB):
                est[k * (HALO // SUB) + h, pl.ds(j * chunk * SUB, chunk * SUB), :] = acc[
                    :, h * SUB:(h + 1) * SUB, :
                ].reshape(chunk * SUB, width)
            esto[0, pl.ds(j * chunk, chunk), k * HALO:(k + 1) * HALO, :] = acc.astype(BF16)
            return c

        lax.fori_loop(0, height // chunk, first, 0)

    est_x[0][0]()
    tables(wxb, ykb, zb, 1, 4, 7, planes, zb.shape[2])

    pairs = height // 2
    fgroups = wide * HALO // SUB

    def yx(yk, wx, v, base, gcount, gp):
        ys = []
        for t in range(terms):
            i = base + t * gcount + 2 * gp
            rhs = jnp.concatenate([zin[i], zin[i + 1]], axis=1)
            ys.append(dot(yk[v * terms + t], rhs).astype(BF16))
        res = []
        for h in range(2):
            lhs = jnp.concatenate([y[:, h * width:(h + 1) * width] for y in ys], axis=1)
            res.append(dot(lhs, wx[v]))
        return res

    for it in range(ITERS):
        est_x[it][1]()

        def zforward(p, c):
            cols = []
            for h in range(2):
                y = 2 * p + h
                cols.append(jnp.concatenate([estp[it, y], esto[it, y], estn[it, y]], axis=0))
            rhs = jnp.concatenate(cols, axis=1)
            r = dot(zf[...].reshape(-1, zf.shape[2]), rhs)
            r = r.reshape(vt * fgroups, SUB, 2 * width)
            r = jnp.concatenate([r[:, :, :width], r[:, :, width:]], axis=1)
            zin[:, pl.ds(pl.multiple_of(p * 2 * SUB, 2 * SUB), 2 * SUB), :] = r.astype(BF16)
            return c

        lax.fori_loop(0, pairs, zforward, 0)

        def forward(gps):
            def one(v, c):
                s = scl[pl.ds(v, 1), :].reshape(1, 1, width)
                for gp in gps:
                    res = yx(ykf, wxf, v, v * terms * fgroups, fgroups, gp)
                    b = jnp.concatenate([x.reshape(height, SUB, width) for x in res], axis=1)
                    q = s * raw[v, gp].astype(F32) / b
                    if gp == 0:
                        q = jnp.where(has_prev, q, 0.0)
                    if gp == wide - 1:
                        q = jnp.where(has_next, q, 0.0)
                    qx[v, gp] = q.astype(BF16)
                return c

            lax.fori_loop(0, views, one, 0)

        forward(range(1, wide - 1))
        if it == 0:
            raw_x[1]()
        forward((0, wide - 1))

        def zbackward(v, c):
            for p in range(pairs):
                cols = [
                    jnp.concatenate([qx[v, g, 2 * p + h] for g in range(wide)], axis=0)
                    for h in range(2)
                ]
                r = dot(zb[v], jnp.concatenate(cols, axis=1))
                r = r.reshape(terms * groups, SUB, 2 * width)
                r = jnp.concatenate([r[:, :, :width], r[:, :, width:]], axis=1)
                zin[pl.ds(v * terms * groups, terms * groups), p * 2 * SUB:(p + 1) * 2 * SUB, :] = (
                    r.astype(BF16)
                )
            return c

        lax.fori_loop(0, views, zbackward, 0)
        fac[...] = jnp.ones_like(fac)

        def backward(v, c):
            for gp in range(own):
                res = yx(ykb, wxb, v, v * terms * groups, groups, gp)
                for h in range(2):
                    fac[2 * gp + h] = fac[2 * gp + h] * res[h]
            return c

        lax.fori_loop(0, views, backward, 0)

        for k in range(own):
            parts = []
            for h in range(2):
                g = 2 * k + h
                new = est[g] * fac[g]
                est[g] = new
                parts.append(new.reshape(height, SUB, width))
            if it + 1 < ITERS:
                esto[it + 1, :, k * HALO:(k + 1) * HALO, :] = jnp.concatenate(
                    parts, axis=1
                ).astype(BF16)
        if it + 1 < ITERS:
            est_x[it + 1][0]()

    for g in range(groups):
        for z in range(SUB):
            out[g * SUB + z] = est[g, pl.ds(z, height, stride=SUB), :]

    raw_x[2]()
    for it in range(ITERS):
        est_x[it][2]()


def local(n, raw_views, spread_taps):
    views, planes, height, width = raw_views.shape
    terms, tap_count = spread_taps.shape[1], spread_taps.shape[3]
    radius = (tap_count - 1) // 2
    vt = views * terms
    taps = spread_taps.astype(BF16).transpose(2, 0, 1, 3).reshape(3 * vt, tap_count)
    taps = jnp.pad(taps, ((0, 0), (0, width - tap_count)))
    own = planes // HALO
    wide = own + 2
    area = SUB * height
    slab = (ITERS, height, planes, width)
    scratch = [
        pltpu.VMEM((planes * height, width), F32),
        pltpu.VMEM((views, wide, height, HALO, width), BF16),
        pltpu.VMEM(slab, BF16),
        pltpu.VMEM(slab, BF16),
        pltpu.VMEM(slab, BF16),
        pltpu.VMEM((planes // SUB, area, width), F32),
        pltpu.VMEM((planes // SUB, area, width), F32),
        pltpu.VMEM((vt * wide * HALO // SUB, area, width), BF16),
        pltpu.VMEM((views, wide, height, HALO, width), BF16),
        pltpu.VMEM((views, terms * width, width), BF16),
        pltpu.VMEM((views, terms * width, width), BF16),
        pltpu.VMEM((vt, area, area), BF16),
        pltpu.VMEM((vt, area, area), BF16),
        pltpu.VMEM((views, terms * wide * HALO, 3 * planes), BF16),
        pltpu.VMEM((views, terms * planes, wide * HALO), BF16),
        pltpu.VMEM((8, vt, width), F32),
        pltpu.VMEM((n, views, width), F32),
        pltpu.VMEM((views, width), F32),
        pltpu.SemaphoreType.DMA((n,)),
        pltpu.SemaphoreType.DMA((n,)),
        pltpu.SemaphoreType.DMA((2,)),
        pltpu.SemaphoreType.DMA((2,)),
        pltpu.SemaphoreType.DMA((ITERS, 2)),
        pltpu.SemaphoreType.DMA((ITERS, 2)),
    ]
    return pl.pallas_call(
        functools.partial(kernel_body, n, radius),
        out_shape=jax.ShapeDtypeStruct((planes, height, width), F32),
        in_specs=[pl.BlockSpec(memory_space=pltpu.VMEM)] * 2,
        out_specs=pl.BlockSpec(memory_space=pltpu.VMEM),
        scratch_shapes=scratch,
        compiler_params=pltpu.CompilerParams(
            collective_id=0, has_side_effects=True, vmem_limit_bytes=56 * 1024 * 1024
        ),
    )(raw_views, taps)


def solution(mesh):
    return jax.shard_map(
        functools.partial(local, mesh.shape["tile"]),
        mesh=mesh,
        in_specs=(P(None, ("blocks", "tile"), None, None), P()),
        out_specs=P(("blocks", "tile"), None, None),
        check_vma=False,
    )
```

```python
import functools

import jax
import jax.numpy as jnp
from jax import lax
from jax.experimental import pallas as pl
from jax.experimental.pallas import tpu as pltpu
from jax.sharding import PartitionSpec as P

ITERS = 2
SUB = 8
HALO = 16
F32 = jnp.float32
BF16 = jnp.bfloat16
MESH = pl.DeviceIdType.MESH


def dot(a, b):
    return jnp.dot(a, b, preferred_element_type=F32)


def kernel_body(
    n, radius, raw_in, taps_in, out, taps, raw, ext, est, fac, zin, zin2, qx,
    wxf, wxb, ykf, ykb, zf, zb, brow, tot, scl,
    tot_ss, tot_rs, raw_ss, raw_rs, est_ss, est_rs,
):
    views, planes, height, width = raw_in.shape
    terms = taps_in.shape[1]
    dims = taps_in.shape[2]
    me = lax.axis_index("tile")
    prev, nxt = lax.rem(me + n - 1, n), lax.rem(me + 1, n)
    has_prev, has_next = me > 0, me < n - 1
    groups = planes // SUB
    own = planes // HALO
    wide = own + 2

    barrier = pltpu.get_barrier_semaphore()

    def greet(i, c):
        pl.semaphore_signal(
            barrier, inc=1, device_id={"tile": lax.rem(me + i, n)}, device_id_type=MESH
        )
        return c

    lax.fori_loop(1, n, greet, 0)

    pl.semaphore_wait(barrier, n - 1)

    def exchange(src_lo, dst_lo, src_hi, dst_hi, ss, rs):
        down = functools.partial(
            pltpu.make_async_remote_copy,
            src_ref=src_lo, dst_ref=dst_hi, send_sem=ss.at[0], recv_sem=rs.at[0],
            device_id={"tile": prev}, device_id_type=MESH,
        )
        up = functools.partial(
            pltpu.make_async_remote_copy,
            src_ref=src_hi, dst_ref=dst_lo, send_sem=ss.at[1], recv_sem=rs.at[1],
            device_id={"tile": nxt}, device_id_type=MESH,
        )
        return down, up

    def raw_copies(v):
        return exchange(
            raw.at[v, 1], raw.at[v, 0], raw.at[v, own], raw.at[v, own + 1],
            raw_ss.at[v], raw_rs.at[v],
        )

    def est_copies(it, k):
        return exchange(
            ext.at[it, own + k], ext.at[it, k], ext.at[it, own + k], ext.at[it, 2 * own + k],
            est_ss.at[it, k], est_rs.at[it, k],
        )

    def start_down(copies):
        @pl.when(has_prev)
        def _():
            copies[0]().start()

    def start_up(copies):
        @pl.when(has_next)
        def _():
            copies[1]().start()

    def wait_hi(copies):
        @pl.when(has_next)
        def _():
            copies[0]().wait_recv()

    def wait_lo(copies):
        @pl.when(has_prev)
        def _():
            copies[1]().wait_recv()

    def wait_sent(copies):
        @pl.when(has_prev)
        def _():
            copies[0]().wait_send()

        @pl.when(has_next)
        def _():
            copies[1]().wait_send()

    area = SUB * height
    pr = lax.broadcasted_iota(jnp.int32, (area, area), 0)
    pc = lax.broadcasted_iota(jnp.int32, (area, area), 1)
    perm = (pc == (pr % SUB) * height + pr // SUB).astype(F32).astype(BF16)
    ahead = views // 2

    def relayout(v):
        total = jnp.zeros((1, 2 * width), F32)
        for k in range(own):
            halves = [
                raw_in[v, k * HALO + h * SUB:k * HALO + (h + 1) * SUB].reshape(area, width)
                for h in range(2)
            ]
            o = dot(perm, jnp.concatenate(halves, axis=1))
            total = total + jnp.sum(o, axis=0, keepdims=True)
            o = o.reshape(height, SUB, 2 * width)
            raw[v, 1 + k] = jnp.concatenate(
                [o[:, :, :width], o[:, :, width:]], axis=1
            ).astype(BF16)
        tot[0, pl.ds(v, 1), :] = total[:, :width] + total[:, width:]

    def relayout_send(v, c):
        relayout(v)
        start_down(raw_copies(v))
        start_up(raw_copies(v))
        return c

    def relayout_only(v, c):
        relayout(v)
        return c

    lax.fori_loop(0, ahead, relayout_send, 0)
    lax.fori_loop(ahead, views, relayout_only, 0)

    def tot_copy(i):
        return pltpu.make_async_remote_copy(
            src_ref=tot.at[0], dst_ref=tot.at[i], send_sem=tot_ss.at[i], recv_sem=tot_rs.at[i],
            device_id={"tile": lax.rem(me + i, n)}, device_id_type=MESH,
        )

    def tot_start(i, c):
        tot_copy(i).start()
        return c

    def tot_wait(i, c):
        tot_copy(i).wait()
        return c

    lax.fori_loop(1, n, tot_start, 0)

    @pl.when(me == 0)
    def _():
        ext[:, 0:own] = jnp.zeros_like(ext[:, 0:own])
        raw[:, 0] = jnp.zeros_like(raw[:, 0])

    @pl.when(me == n - 1)
    def _():
        ext[:, 2 * own:] = jnp.zeros_like(ext[:, 2 * own:])
        raw[:, own + 1] = jnp.zeros_like(raw[:, own + 1])

    taps[...] = jnp.zeros_like(taps)
    for v in range(views):
        for t in range(terms):
            at = (v * terms + t) * dims
            taps[at:at + dims, 0:taps_in.shape[3]] = taps_in[v, t]
    rounded_taps = taps[...].astype(BF16)

    lanes = taps.shape[1]
    tap = lax.broadcasted_iota(jnp.int32, (lanes, lanes), 0)
    lane = lax.broadcasted_iota(jnp.int32, (lanes, lanes), 1)
    signed = jnp.where(lane < lanes // 2, lane, lane - lanes)
    far = lane - lanes
    vt = views * terms

    def place(k, wanted, keep=None):
        hit = tap == wanted
        if keep is not None:
            hit = jnp.logical_and(hit, keep)
        brow[k] = dot(rounded_taps, hit.astype(F32).astype(BF16))

    step = lane % SUB == 0
    place(0, radius - signed)
    place(1, radius + signed)
    place(2, lane // SUB + radius, step)
    place(3, lane // SUB + radius - lanes // SUB, step)
    place(4, radius - lane // SUB, step)
    place(5, radius - lane // SUB + lanes // SUB, step)
    place(6, lane - (HALO - radius))
    place(7, 2 * radius + HALO - radius - lane)

    row = tap
    near = jnp.abs(row - lane) <= radius
    after = lane >= row

    def rolled(k, i, rows):
        line = jnp.broadcast_to(brow[k, pl.ds(dims * i[0] + i[1], 1), :], (rows, lanes))
        return pltpu.roll(line, 0, 1, stride=1, stride_axis=0)

    def tables(wx, yk, z, kx, ky, kz, zrows, zcols):
        def one(v, c):
            for t in range(terms):
                i = v * terms + t
                wx[v, t * width:(t + 1) * width, :] = jnp.where(
                    near, rolled(kx, (i, 2), width), 0.0
                ).astype(BF16)
                r0 = rolled(ky, (i, 1), lanes)
                r1 = rolled(ky + 1, (i, 1), lanes)
                t0 = jnp.where(after, r0, r1).astype(BF16)
                yk[i, 0:lanes, 0:lanes] = t0
                yk[i, lanes:2 * lanes, lanes:2 * lanes] = t0
                yk[i, 0:lanes, lanes:2 * lanes] = jnp.where(after, 0.0, r0).astype(BF16)
                yk[i, lanes:2 * lanes, 0:lanes] = jnp.where(after, r1, 0.0).astype(BF16)
                z[v, t * zrows:(t + 1) * zrows, :] = rolled(kz, (i, 0), zrows)[:, :zcols].astype(BF16)
            return c

        lax.fori_loop(0, views, one, 0)

    tables(wxf, ykf, zf, 0, 2, 6, HALO, zf.shape[2])

    lax.fori_loop(1, n, tot_wait, 0)
    summed = lax.fori_loop(0, n, lambda i, a: a + tot[i], jnp.zeros(tot.shape[1:], F32))
    totals = jnp.sum(summed, axis=1, keepdims=True)
    mean = jnp.sum(totals, axis=0, keepdims=True) / views
    scl[...] = jnp.broadcast_to(mean / totals, scl.shape)

    chunk = SUB
    for k in range(own):
        def first(j, c):
            acc = jnp.zeros((chunk, HALO, width), F32)
            for v in range(views):
                s = scl[v:v + 1, :].reshape(1, 1, width)
                acc = acc + s * raw[v, 1 + k, pl.ds(j * chunk, chunk)].astype(F32)
            acc = acc / views
            for h in range(HALO // SUB):
                est[k * (HALO // SUB) + h, pl.ds(j * chunk * SUB, chunk * SUB), :] = acc[
                    :, h * SUB:(h + 1) * SUB, :
                ].reshape(chunk * SUB, width)
            ext[0, own + k, pl.ds(j * chunk, chunk)] = acc.astype(BF16)
            return c

        lax.fori_loop(0, height // chunk, first, 0)

    def send_est(it, k):
        copies = est_copies(it, k)
        if k < own // 2:
            start_down(copies)
            start_up(copies)
        else:
            start_up(copies)
            start_down(copies)

    for k in range(own):
        send_est(0, k)

    def raw_start(v, c):
        start_down(raw_copies(v))
        start_up(raw_copies(v))
        return c

    lax.fori_loop(ahead, views, raw_start, 0)
    tables(wxb, ykb, zb, 1, 4, 7, planes, zb.shape[2])

    pairs = height // 2

    def yx(yk, wx, z, v, first, step):
        ys = []
        for t in range(terms):
            i = first + t * step
            rhs = jnp.concatenate([z[i], z[i + 1]], axis=1)
            ys.append(dot(yk[v * terms + t], rhs).astype(BF16))
        lhs = jnp.concatenate(
            [
                jnp.concatenate([y[:, h * width:(h + 1) * width] for y in ys], axis=1)
                for h in range(2)
            ],
            axis=0,
        )
        res = dot(lhs, wx[v])
        return [res[h * area:(h + 1) * area] for h in range(2)]

    order = list(range(own, 0, -1)) + [own + 1, 0]
    for it in range(ITERS):
        def forward(gp):
            def zforward(p, c):
                cols = [
                    jnp.concatenate(
                        [ext[it, own + gp - 2 + d, 2 * p + h] for d in range(3)], axis=0
                    )
                    for h in range(2)
                ]
                rhs = jnp.concatenate(cols, axis=1)
                r = dot(zf[...].reshape(-1, zf.shape[2]), rhs)
                r = r.reshape(vt * 2, SUB, 2 * width)
                r = jnp.concatenate([r[:, :, :width], r[:, :, width:]], axis=1)
                at = pl.ds(pl.multiple_of(p * 2 * SUB, 2 * SUB), 2 * SUB)
                zin[:, at, :] = r.astype(BF16)
                return c

            lax.fori_loop(0, pairs, zforward, 0, unroll=2)

            def one(v, c):
                s = scl[pl.ds(v, 1), :].reshape(1, 1, width)
                if it == 0 and gp == 0:
                    wait_lo(raw_copies(v))
                if it == 0 and gp == wide - 1:
                    wait_hi(raw_copies(v))
                res = yx(ykf, wxf, zin, v, v * terms * 2, 2)
                b = jnp.concatenate([x.reshape(height, SUB, width) for x in res], axis=1)
                q = s * raw[v, gp].astype(F32) / b
                if gp == 0:
                    q = jnp.where(has_prev, q, 0.0)
                if gp == wide - 1:
                    q = jnp.where(has_next, q, 0.0)
                qx[v, gp] = q.astype(BF16)
                return c

            lax.fori_loop(0, views, one, 0, unroll=1 if it == 0 and gp in (0, wide - 1) else 4)

        for gp in order:
            if gp == own:
                wait_hi(est_copies(it, 0))
            if gp == 1:
                wait_lo(est_copies(it, own - 1))
            if gp == wide - 1:
                for k in range(1, own):
                    wait_hi(est_copies(it, k))
            if gp == 0:
                for k in range(own - 1):
                    wait_lo(est_copies(it, k))
            forward(gp)

        def zbackward(v, c):
            for p in range(pairs):
                cols = [
                    jnp.concatenate([qx[v, g, 2 * p + h] for g in range(wide)], axis=0)
                    for h in range(2)
                ]
                r = dot(zb[v], jnp.concatenate(cols, axis=1))
                r = r.reshape(terms * groups, SUB, 2 * width)
                r = jnp.concatenate([r[:, :, :width], r[:, :, width:]], axis=1)
                zin2[pl.ds(v * terms * groups, terms * groups), p * 2 * SUB:(p + 1) * 2 * SUB, :] = (
                    r.astype(BF16)
                )
            return c

        lax.fori_loop(0, views, zbackward, 0)
        fac[...] = jnp.ones_like(fac)

        for k in range(own):
            def backward(v, c):
                res = yx(ykb, wxb, zin2, v, v * terms * groups + 2 * k, groups)
                for h in range(2):
                    fac[2 * k + h] = fac[2 * k + h] * res[h]
                return c

            lax.fori_loop(0, views, backward, 0, unroll=4)
            parts = []
            for h in range(2):
                g = 2 * k + h
                new = est[g] * fac[g]
                est[g] = new
                parts.append(new.reshape(height, SUB, width))
            if it + 1 < ITERS:
                ext[it + 1, own + k] = jnp.concatenate(parts, axis=1).astype(BF16)
                send_est(it + 1, k)

    for g in range(groups):
        for z in range(SUB):
            out[g * SUB + z] = est[g, pl.ds(z, height, stride=SUB), :]

    def raw_sent(v, c):
        wait_sent(raw_copies(v))
        return c

    lax.fori_loop(0, views, raw_sent, 0)
    for it in range(ITERS):
        for k in range(own):
            wait_sent(est_copies(it, k))


def local(n, raw_views, spread_taps):
    views, planes, height, width = raw_views.shape
    terms, tap_count = spread_taps.shape[1], spread_taps.shape[3]
    radius = (tap_count - 1) // 2
    vt = views * terms
    own = planes // HALO
    wide = own + 2
    area = SUB * height
    scratch = [
        pltpu.VMEM((3 * vt, width), F32),
        pltpu.VMEM((views, wide, height, HALO, width), BF16),
        pltpu.VMEM((ITERS, 3 * own, height, HALO, width), BF16),
        pltpu.VMEM((planes // SUB, area, width), F32),
        pltpu.VMEM((planes // SUB, area, width), F32),
        pltpu.VMEM((vt * HALO // SUB, area, width), BF16),
        pltpu.VMEM((vt * planes // SUB, area, width), BF16),
        pltpu.VMEM((views, wide, height, HALO, width), BF16),
        pltpu.VMEM((views, terms * width, width), BF16),
        pltpu.VMEM((views, terms * width, width), BF16),
        pltpu.VMEM((vt, area, area), BF16),
        pltpu.VMEM((vt, area, area), BF16),
        pltpu.VMEM((views, terms * HALO, 3 * HALO), BF16),
        pltpu.VMEM((views, terms * planes, wide * HALO), BF16),
        pltpu.VMEM((8, 3 * vt, width), F32),
        pltpu.VMEM((n, views, width), F32),
        pltpu.VMEM((views, width), F32),
        pltpu.SemaphoreType.DMA((n,)),
        pltpu.SemaphoreType.DMA((n,)),
        pltpu.SemaphoreType.DMA((views, 2)),
        pltpu.SemaphoreType.DMA((views, 2)),
        pltpu.SemaphoreType.DMA((ITERS, own, 2)),
        pltpu.SemaphoreType.DMA((ITERS, own, 2)),
    ]
    return pl.pallas_call(
        functools.partial(kernel_body, n, radius),
        out_shape=jax.ShapeDtypeStruct((planes, height, width), F32),
        in_specs=[pl.BlockSpec(memory_space=pltpu.VMEM)] * 2,
        out_specs=pl.BlockSpec(memory_space=pltpu.VMEM),
        scratch_shapes=scratch,
        compiler_params=pltpu.CompilerParams(
            collective_id=0, has_side_effects=True, vmem_limit_bytes=56 * 1024 * 1024
        ),
    )(raw_views, spread_taps)


def solution(mesh):
    return jax.shard_map(
        functools.partial(local, mesh.shape["tile"]),
        mesh=mesh,
        in_specs=(P(None, ("blocks", "tile"), None, None), P()),
        out_specs=P(("blocks", "tile"), None, None),
        check_vma=False,
    )
```
